32 devices in a mesh: rep: 4 (over x, core), fsdp: 8 (over z, y).
Axes of the slice: x: 2, y: 2, z: 4, core: 2. Of those that a mesh axis runs over, the one named last changes fastest.
Arguments:
- tokens: bfloat16 [8192, 4096], P(('rep', 'fsdp')), may hold values from -6 to 6
- cotangent: bfloat16 [8192, 512], P(('rep', 'fsdp')), may hold values from -0.0625 to 0.0625
- momentum: float32 [4, 4096, 512], P('rep', 'fsdp'), may hold values from -6 to 6
- weight: bfloat16 [4096, 512], P('fsdp'), may hold values from -0.09375 to 0.09375
- picks: int32 [4, 512, 32], P(None, 'fsdp'), may hold values from 0 to 4095, as said below
- next_tokens: bfloat16 [4096, 4096], P(('rep', 'fsdp')), may hold values from -3 to 3
Outputs:
- momentum_out: float32 [4, 4096, 512], P('rep', 'fsdp')
- next_keys: float32 [4096, 512], P(('rep', 'fsdp'))
The draws below stay inside these ranges and needn't reach their ends.
Inputs may be any that keep to these rules, and one draw needn't show every extreme that they name: `picks`: for each replica and tile the 32 positions are distinct.
All inputs are finite; a program needn't handle non-finite values.
Results may differ from the reference program's by a relative error of at most 0.014.
Values may be sent and summed in bfloat16 or wider, within the bound.
A program may use at most 64 MiB of HBM per device.

```python
import math
import jax
import jax.numpy as jnp
from jax import lax

TILE = 64
D_WIN = 4096
KV_WIN = 512
TOPK = 32
TOK_DEV = 256
TILES = 512
TOKENS = 8192
NEXT_TOKENS = 4096
N_REP = 4
N_FSDP = 8


def draw_picks(key, part):
    key = jax.random.fold_in(key, 7)
    positions = TILE * TILE

    def per_replica(replica):
        subkey = jax.random.fold_in(key, replica)
        scores = jax.random.randint(subkey, (TILES, positions), 0, 2 ** 18) * positions
        scores = scores + jnp.arange(positions, dtype=jnp.int32)[None, :]
        return lax.top_k(scores, TOPK)[1].astype(jnp.int32)
    return lax.map(per_replica, jnp.arange(N_REP, dtype=jnp.int32))


def levels(stream_key, shape, split, smallest, top_value):
    gain, own = 1.0, jax.random.fold_in(stream_key, 6)
    for axis_at, blocks in split:
        draws = jnp.exp(jax.random.uniform(jax.random.fold_in(own, axis_at), (blocks,), jnp.float32, smallest / len(split), top_value / len(split)))
        gain = gain * jnp.repeat(draws, shape[axis_at] // blocks).reshape([-1 if axis == axis_at else 1 for axis in range(len(shape))])
    return gain


def scatter_about(key, shape, width, most, cuts=(), kind=jnp.bfloat16):
    factor_of = levels(key, shape, cuts, -0.22, 0.18) if cuts else 1.0
    values = jax.random.normal(key, shape, jnp.float32) * width * factor_of
    return jnp.minimum(jnp.maximum(values, -most), most).astype(kind)


def setup_inputs(seed: int = 0) -> dict:
    splits = jax.random.split(jax.random.key(seed), 7)
    tokens = scatter_about(splits[0], (TOKENS, D_WIN), 1.0, 6.0, ((0, 32),))
    cotangent = scatter_about(splits[1], (TOKENS, KV_WIN), (4 * TOK_DEV * N_FSDP) ** -0.5, 0.0625, ((0, 32),))
    momentum = scatter_about(splits[2], (N_REP, D_WIN, KV_WIN), 1.0, 6.0, ((0, 4), (1, 8)), jnp.float32)
    weight = scatter_about(splits[3], (D_WIN, KV_WIN), D_WIN ** -0.5, 0.09375, ((0, 8),))
    picks = draw_picks(jax.random.fold_in(splits[6], 71), 0)
    next_tokens = scatter_about(splits[5], (NEXT_TOKENS, D_WIN), 0.5, 3.0, ((0, 32),))
    return dict(tokens=tokens, cotangent=cotangent, momentum=momentum, weight=weight, picks=picks, next_tokens=next_tokens)


decay_rate = 0.999
step_size = 0.02

def cosine_block(length, tile_len):
    freq_ids = jnp.arange(length, dtype=jnp.int32)[:, None]
    cell_ids = jnp.arange(length, dtype=jnp.int32)[None, :]
    freqs = (freq_ids % tile_len).astype(jnp.float32)
    cells = (cell_ids % tile_len).astype(jnp.float32)
    values = jnp.cos(math.pi * (2.0 * cells + 1.0) * freqs / (2.0 * tile_len)) * math.sqrt(2.0 / tile_len)
    values = jnp.where(freqs == 0.0, values * math.sqrt(0.5), values)
    same_block = freq_ids // tile_len == cell_ids // tile_len
    return jnp.where(same_block, values, jnp.zeros_like(values)).astype(jnp.float32)

def flat_positions(picks, col_count):
    tile_cols = col_count // TILE
    tile_ids = jnp.arange(picks.shape[-2], dtype=jnp.int32)[:, None]
    row_ids = tile_ids // tile_cols * TILE + picks // TILE
    col_ids = tile_ids % tile_cols * TILE + picks % TILE
    return (row_ids * col_count + col_ids).astype(jnp.int32)

def tile_view(matrix):
    row_count, col_count = matrix.shape
    return matrix.reshape(row_count // TILE, TILE, col_count // TILE, TILE)

def forward_tiles(matrix, cosines):
    tiles = tile_view(matrix)
    result = jnp.einsum('ji,aibk,lk->ajbl', cosines, tiles, cosines, precision=lax.Precision.HIGHEST)
    return result.reshape(matrix.shape)

def inverse_tiles(matrix, cosines):
    tiles = tile_view(matrix)
    result = jnp.einsum('ji,ajbl,lk->aibk', cosines, tiles, cosines, precision=lax.Precision.HIGHEST)
    return result.reshape(matrix.shape)

def reference(tokens, cotangent, momentum, weight, picks, next_tokens):
    row_count, col_count = weight.shape
    cosines = cosine_block(TILE, TILE)
    flat_index = flat_positions(picks, col_count)
    token_blocks = tokens.reshape(N_REP, N_FSDP, TOK_DEV, row_count)
    cot_blocks = cotangent.reshape(N_REP, N_FSDP, TOK_DEV, col_count)

    def per_replica(running, inputs):
        token_rep, cot_rep, moment_rep, flat_rep = inputs

        def add_block(acc, blocks_pair):
            partial_term = lax.dot_general(blocks_pair[0], blocks_pair[1], (((0,), (0,)), ((), ())), preferred_element_type=jnp.float32)
            rounded = lax.optimization_barrier(partial_term.astype(jnp.bfloat16))
            return (acc + rounded.astype(jnp.float32), None)
        grad, _ = lax.scan(add_block, jnp.zeros((row_count, col_count), jnp.float32), (token_rep, cot_rep))
        velocity = decay_rate * moment_rep + grad
        coefs = forward_tiles(velocity, cosines)
        sent_values = jnp.take(coefs.reshape(-1), flat_rep)
        own_sparse = jnp.zeros((row_count * col_count,), jnp.float32).at[flat_rep.reshape(-1)].add(sent_values.reshape(-1)).reshape(row_count, col_count)
        moment_new = velocity - inverse_tiles(own_sparse, cosines)
        return (running + own_sparse, moment_new)
    summed, momentum_out = lax.scan(per_replica, jnp.zeros((row_count, col_count), jnp.float32), (token_blocks, cot_blocks, momentum, flat_index))
    update = inverse_tiles(summed, cosines)
    new_weight = (weight.astype(jnp.float32) - step_size * update).astype(jnp.bfloat16)
    next_keys = jnp.dot(next_tokens, new_weight, preferred_element_type=jnp.float32)
    return (momentum_out, next_keys)
```

```python
import functools
import math

import jax
import jax.numpy as jnp
import numpy as np
from jax import lax
from jax.experimental import pallas as pl
from jax.experimental.pallas import tpu as pltpu
from jax.sharding import PartitionSpec as P

TILE = 64
LANES = 2 * TILE
decay_rate = 0.999
step_size = 0.02
MESH = pl.DeviceIdType.MESH
F32 = jnp.float32
BF16 = jnp.bfloat16


def cosine_parts():
    freq = np.arange(TILE)[None, :]
    cell = np.arange(TILE)[:, None]
    table = np.cos(math.pi * (2 * cell + 1) * freq / (2 * TILE)) * math.sqrt(2 / TILE)
    table = np.where(freq == 0, table * math.sqrt(0.5), table).astype(np.float32)
    head = table.astype(BF16)
    tail = (table - head.astype(np.float32)).astype(BF16)
    return np.concatenate([head, tail, head], axis=0)


def halves(x):
    head = x.astype(BF16)
    return head, (x - head.astype(F32)).astype(BF16)


def dot_tn(a, b):
    return lax.dot_general(a, b, (((0,), (0,)), ((), ())), preferred_element_type=F32)


def dot_nt(a, b):
    return lax.dot_general(a, b, (((1,), (1,)), ((), ())), preferred_element_type=F32)


def kernel(
    n_rep, n_fsdp,
    tokens, cot, moment, weight, picks, next_tokens, table,
    moment_out, keys_out,
    own_tok, mate_tok, mate_cot, line_in, line_out, acc,
    vel, rows3, cols_hi, cols_lo, own_vals, peer_vals,
    new_weight, next_in, pair_out, pair_in, key_in, key_out,
    local_sem, cot_sems, tok_send, tok_recv, line_send, line_recv,
    val_send, val_recv, next_send, next_recv, pair_send, pair_recv,
    key_send, key_recv,
):
    groups = n_fsdp // 2
    rep = lax.axis_index("rep")
    me = lax.axis_index("fsdp")
    side = lax.rem(me, 2)
    place = me // 2
    mate = me + 1 - 2 * side
    rows, cols = weight.shape
    pairs, width = picks.shape
    per_tile = width // 2
    kept = per_tile // n_rep
    across = cols // LANES

    barrier = pltpu.get_barrier_semaphore()
    for step in range(1, n_fsdp):
        pl.semaphore_signal(
            barrier, inc=1, device_id={"fsdp": lax.rem(me + step, n_fsdp)}, device_id_type=MESH
        )
    for step in range(1, n_rep):
        pl.semaphore_signal(
            barrier, inc=1, device_id={"rep": lax.rem(rep + step, n_rep)}, device_id_type=MESH
        )
    pl.semaphore_wait(barrier, n_fsdp + n_rep - 2)

    def block(owner):
        return pl.ds(pl.multiple_of(owner * rows, rows), rows)

    def remote(src, dst, send, recv, **device):
        return pltpu.make_async_remote_copy(
            src_ref=src, dst_ref=dst, send_sem=send, recv_sem=recv,
            device_id=device, device_id_type=MESH,
        )

    def each_event(body):
        def step(event, carry):
            way = lax.rem(event, 2)
            turn = event // 2
            group = way * turn + (1 - way) * (groups - 1 - turn)
            active = ((way == 0) & (place < group)) | ((way == 1) & (place > group))

            @pl.when(active)
            def _():
                body(way, group)

            return carry

        lax.fori_loop(0, 2 * (groups - 1), step, 0)

    def cot_copy():
        return remote(cot, mate_cot, cot_sems.at[0], cot_sems.at[1], fsdp=mate)

    def tok_copy(group):
        return remote(
            tokens.at[:, block(2 * group + 1 - side)], mate_tok.at[group],
            tok_send.at[group], tok_recv.at[group], fsdp=mate,
        )

    def tok_local(group):
        return pltpu.make_async_copy(
            tokens.at[:, block(2 * group + side)], own_tok.at[group], local_sem.at[group]
        )

    def next_copy(step):
        target = lax.rem(me + step, n_fsdp)
        return remote(
            next_tokens.at[:, block(target)], next_in.at[me],
            next_send.at[step], next_recv.at[me], fsdp=target,
        )

    def next_wait(source):
        return remote(
            next_tokens.at[:, block(me)], next_in.at[source],
            next_send.at[0], next_recv.at[source], fsdp=mate,
        )

    def next_local():
        return pltpu.make_async_copy(
            next_tokens.at[:, block(me)], next_in.at[me], local_sem.at[groups]
        )

    cot_copy().start()
    each_event(lambda way, group: tok_copy(group).start())
    tok_copy(place).start()
    each_event(lambda way, group: tok_local(group).start())
    tok_local(place).start()
    next_local().start()
    for step in range(1, n_fsdp):
        next_copy(step).start()

    def name_rows(pair, carry):
        spots = picks[pl.ds(pair, 1), :]
        ids = lax.broadcasted_iota(jnp.int32, (TILE, width), 0)
        pick_row = jnp.where(ids == spots // TILE, 1.0, 0.0).astype(BF16)
        pick_col = jnp.where(ids == lax.rem(spots, TILE), 1.0, 0.0).astype(BF16)
        rows3[pair] = jnp.dot(table[...], pick_row, preferred_element_type=F32).astype(BF16)
        found = jnp.dot(
            table[pl.ds(0, LANES), :], pick_col, preferred_element_type=F32
        )
        first = lax.broadcasted_iota(jnp.int32, (TILE, width), 1) < per_tile
        for part, target in ((found[:TILE], cols_hi), (found[TILE:], cols_lo)):
            target[pair] = jnp.concatenate(
                [jnp.where(first, part, 0.0), jnp.where(first, 0.0, part)], axis=0
            ).astype(BF16)
        return carry

    lax.fori_loop(0, pairs, name_rows, 0)

    def line_copy(way, group, source, target, send, recv):
        return remote(
            source.at[group], target.at[way, group], send.at[group], recv.at[way, group],
            fsdp=lax.rem(me + 2 - 4 * way + n_fsdp, n_fsdp),
        )

    def line_reduce(term, total, source, target, send, recv):
        def take(way, group):
            line_copy(way, group, source, target, send, recv).wait_recv()
            total[...] += target[way, group].astype(F32)

        def handle(way, group):
            total[...] = term(group)

            @pl.when(((way == 0) & (place > 0)) | ((way == 1) & (place < groups - 1)))
            def _():
                take(way, group)

            source[group] = total[...].astype(BF16)
            line_copy(way, group, source, target, send, recv).start()

        each_event(handle)
        total[...] = term(place)

        @pl.when(place > 0)
        def _():
            take(0, place)

        @pl.when(place < groups - 1)
        def _():
            take(1, place)

    cot_copy().wait_recv()

    def grad_term(group):
        tok_local(group).wait()
        tok_copy(group).wait_recv()
        return dot_tn(own_tok[group], cot[...]) + dot_tn(mate_tok[group], mate_cot[...])

    line_reduce(grad_term, acc, line_out, line_in, line_send, line_recv)
    vel[...] = decay_rate * moment[0] + acc[...]

    def window(pair):
        top = pl.multiple_of(pair // across * TILE, TILE)
        left = pl.multiple_of(lax.rem(pair, across) * LANES, LANES)
        return pl.ds(top, TILE), pl.ds(left, LANES)

    def coefficients(pair, carry):
        down, over = window(pair)
        head, tail = halves(vel[down, over])
        half = dot_tn(jnp.concatenate([head, head, tail], axis=0), rows3[pair])
        full = cols_hi[pair].astype(F32) + cols_lo[pair].astype(F32)
        found = jnp.sum(half * full, axis=0, keepdims=True)
        lane = lax.broadcasted_iota(jnp.int32, (1, width), 1)
        mine = lax.rem(lane, per_tile) // kept == rep
        own_vals[pl.ds(pair, 1), :] = jnp.where(mine, found, 0.0)
        return carry

    lax.fori_loop(0, pairs, coefficients, 0, unroll=4)

    def val_copy(step):
        return remote(
            own_vals, peer_vals.at[step - 1], val_send.at[step], val_recv.at[step],
            rep=lax.rem(rep + step, n_rep),
        )

    for step in range(1, n_rep):
        val_copy(step).start()

    def inverse(pair, values):
        row_parts = rows3[pair]
        scaled = (row_parts[:TILE].astype(F32) + row_parts[TILE:LANES].astype(F32)) * values
        head, tail = halves(scaled)
        both = dot_nt(jnp.concatenate([head, tail], axis=0), cols_hi[pair])
        return both[:TILE] + both[TILE:] + dot_nt(head, cols_lo[pair])

    def residual(pair, carry):
        down, over = window(pair)
        moment_out[0, down, over] = vel[down, over] - inverse(pair, own_vals[pl.ds(pair, 1), :])
        return carry

    lax.fori_loop(0, pairs, residual, 0, unroll=4)

    for step in range(1, n_rep):
        val_copy(step).wait_recv()

    def renew(pair, carry):
        down, over = window(pair)
        values = own_vals[pl.ds(pair, 1), :]
        for step in range(1, n_rep):
            values += peer_vals[step - 1, pl.ds(pair, 1), :]
        new_weight[down, over] = (
            weight[down, over].astype(F32) - step_size * inverse(pair, values)
        ).astype(BF16)
        return carry

    lax.fori_loop(0, pairs, renew, 0, unroll=4)

    next_local().wait()
    for step in range(1, n_fsdp):
        next_wait(lax.rem(me + n_fsdp - step, n_fsdp)).wait_recv()

    def key_part(owner):
        return jnp.dot(next_in[owner], new_weight[...], preferred_element_type=F32)

    def pair_copy(group):
        return remote(
            pair_out.at[group], pair_in.at[group],
            pair_send.at[group], pair_recv.at[group], fsdp=mate,
        )

    def send_pair(group):
        pair_out[group] = key_part(2 * group + 1 - side).astype(BF16)
        pair_copy(group).start()

    each_event(lambda way, group: send_pair(group))
    send_pair(place)

    def key_term(group):
        own = key_part(2 * group + side)
        pair_copy(group).wait_recv()
        return own + pair_in[group].astype(F32)

    line_reduce(key_term, keys_out, key_out, key_in, key_send, key_recv)

    cot_copy().wait_send()
    for step in range(1, n_fsdp):
        next_copy(step).wait_send()
    for step in range(1, n_rep):
        val_copy(step).wait_send()

    def finish(way, group):
        tok_copy(group).wait_send()
        pair_copy(group).wait_send()
        line_copy(way, group, line_out, line_in, line_send, line_recv).wait_send()
        line_copy(way, group, key_out, key_in, key_send, key_recv).wait_send()

    each_event(finish)
    tok_copy(place).wait_send()
    pair_copy(place).wait_send()


def on_device(n_rep, n_fsdp, tokens, cotangent, momentum, weight, picks, next_tokens):
    groups = n_fsdp // 2
    rows, cols = weight.shape
    count = tokens.shape[0]
    ahead = next_tokens.shape[0]
    tiles, kept = picks.shape[1:]
    pairs, width = tiles // 2, 2 * n_rep * kept
    spots = jnp.transpose(picks, (1, 0, 2)).reshape(pairs, width)
    dma = pltpu.SemaphoreType.DMA
    vmem = pl.BlockSpec(memory_space=pltpu.VMEM)
    hbm = pl.BlockSpec(memory_space=pl.ANY)
    return pl.pallas_call(
        functools.partial(kernel, n_rep, n_fsdp),
        out_shape=(
            jax.ShapeDtypeStruct(momentum.shape, F32),
            jax.ShapeDtypeStruct((ahead, cols), F32),
        ),
        in_specs=[hbm, vmem, vmem, vmem, vmem, hbm, vmem],
        out_specs=(vmem, vmem),
        scratch_shapes=[
            pltpu.VMEM((groups, count, rows), BF16),
            pltpu.VMEM((groups, count, rows), BF16),
            pltpu.VMEM((count, cols), BF16),
            pltpu.VMEM((2, groups, rows, cols), BF16),
            pltpu.VMEM((groups, rows, cols), BF16),
            pltpu.VMEM((rows, cols), F32),
            pltpu.VMEM((rows, cols), F32),
            pltpu.VMEM((pairs, 3 * TILE, width), BF16),
            pltpu.VMEM((pairs, LANES, width), BF16),
            pltpu.VMEM((pairs, LANES, width), BF16),
            pltpu.VMEM((pairs, width), F32),
            pltpu.VMEM((n_rep - 1, pairs, width), F32),
            pltpu.VMEM((rows, cols), BF16),
            pltpu.VMEM((n_fsdp, ahead, rows), BF16),
            pltpu.VMEM((groups, ahead, cols), BF16),
            pltpu.VMEM((groups, ahead, cols), BF16),
            pltpu.VMEM((2, groups, ahead, cols), BF16),
            pltpu.VMEM((groups, ahead, cols), BF16),
            dma((groups + 1,)),
            dma((2,)),
            dma((groups,)),
            dma((groups,)),
            dma((groups,)),
            dma((2, groups)),
            dma((n_rep,)),
            dma((n_rep,)),
            dma((n_fsdp,)),
            dma((n_fsdp,)),
            dma((groups,)),
            dma((groups,)),
            dma((groups,)),
            dma((2, groups)),
        ],
        compiler_params=pltpu.CompilerParams(
            collective_id=0, has_side_effects=True, vmem_limit_bytes=52 * 1024 * 1024
        ),
    )(tokens, cotangent, momentum, weight, spots, next_tokens, jnp.asarray(cosine_parts()))


def solution(mesh):
    placed = (
        P(("rep", "fsdp"), None),
        P(("rep", "fsdp"), None),
        P("rep", "fsdp", None),
        P("fsdp", None),
        P(None, "fsdp", None),
        P(("rep", "fsdp"), None),
    )
    return jax.shard_map(
        functools.partial(on_device, mesh.shape["rep"], mesh.shape["fsdp"]),
        mesh=mesh,
        in_specs=placed,
        out_specs=(P("rep", "fsdp", None), P(("rep", "fsdp"), None)),
        check_vma=False,
    )
```

```python
import functools
import math

import jax
import jax.numpy as jnp
import numpy as np
from jax import lax
from jax.experimental import pallas as pl
from jax.experimental.pallas import tpu as pltpu
from jax.sharding import PartitionSpec as P

TILE = 64
LANES = 2 * TILE
decay_rate = 0.999
step_size = 0.02
MESH = pl.DeviceIdType.MESH
F32 = jnp.float32
BF16 = jnp.bfloat16


def cosine_parts():
    freq = np.arange(TILE)[None, :]
    cell = np.arange(TILE)[:, None]
    table = np.cos(math.pi * (2 * cell + 1) * freq / (2 * TILE)) * math.sqrt(2 / TILE)
    table = np.where(freq == 0, table * math.sqrt(0.5), table).astype(np.float32)
    head = table.astype(BF16)
    tail = (table - head.astype(np.float32)).astype(BF16)
    return np.concatenate([head, tail, head], axis=0)


def halves(x):
    head = x.astype(BF16)
    return head, (x - head.astype(F32)).astype(BF16)


def dot_tn(a, b):
    return lax.dot_general(a, b, (((0,), (0,)), ((), ())), preferred_element_type=F32)


def dot_nt(a, b):
    return lax.dot_general(a, b, (((1,), (1,)), ((), ())), preferred_element_type=F32)


def kernel(
    n_rep, n_fsdp,
    tokens, cot_far, moment_far, weight_far, picks, next_tokens, table,
    moment_out, keys_out,
    cot, moment, weight, own_tok, mate_tok, mate_cot, line_in, line_out, acc,
    vel, rows3, cols_hi, cols_lo, own_vals, peer_vals,
    new_weight, next_in, key_in, key_out,
    near_sem, local_sem, cot_sems, tok_send, tok_recv, line_send, line_recv,
    val_send, val_recv, next_send, next_recv, half_send, half_recv,
    key_send, key_recv,
):
    groups = n_fsdp // 2
    rep = lax.axis_index("rep")
    me = lax.axis_index("fsdp")
    side = lax.rem(me, 2)
    place = me // 2
    mate = me + 1 - 2 * side
    core = lax.rem(rep, 2)
    sibling = rep + 1 - 2 * core
    rows, cols = weight.shape
    kept = picks.shape[2]
    pairs, width = own_vals.shape
    per_tile = width // 2
    across = cols // LANES
    half = rows // 2

    near = [
        pltpu.make_async_copy(far, here, near_sem.at[at])
        for at, (far, here) in enumerate(
            ((cot_far, cot), (moment_far.at[0], moment), (weight_far, weight))
        )
    ]
    for copy in near:
        copy.start()

    def peer(step):
        return 2 * lax.rem(place + step, groups) + side

    barrier = pltpu.get_barrier_semaphore()
    pl.semaphore_signal(barrier, inc=1, device_id={"fsdp": mate}, device_id_type=MESH)
    for step in range(1, groups):
        pl.semaphore_signal(barrier, inc=1, device_id={"fsdp": peer(step)}, device_id_type=MESH)
    for step in range(1, n_rep):
        pl.semaphore_signal(
            barrier, inc=1, device_id={"rep": lax.rem(rep + step, n_rep)}, device_id_type=MESH
        )
    pl.semaphore_wait(barrier, groups + n_rep - 1)

    def block(owner):
        return pl.ds(pl.multiple_of(owner * rows, rows), rows)

    def remote(src, dst, send, recv, **device):
        return pltpu.make_async_remote_copy(
            src_ref=src, dst_ref=dst, send_sem=send, recv_sem=recv,
            device_id=device, device_id_type=MESH,
        )

    above, below = groups - 1 - place, place
    both_ways = jnp.minimum(above, below)

    def order(at):
        way = jnp.where(at < 2 * both_ways, lax.rem(at, 2), jnp.where(above > below, 0, 1))
        turn = jnp.where(at < 2 * both_ways, at // 2, at - both_ways)
        group = jnp.where(way == 0, groups - 1 - turn, turn)
        return way, jnp.where(at == groups - 1, place, group)

    def cot_copy():
        return remote(cot_far, mate_cot, cot_sems.at[0], cot_sems.at[1], fsdp=mate)

    def tok_copy(group):
        return remote(
            tokens.at[:, block(2 * group + 1 - side)], mate_tok.at[group],
            tok_send.at[group], tok_recv.at[group], fsdp=mate,
        )

    def tok_local(group):
        return pltpu.make_async_copy(
            tokens.at[:, block(2 * group + side)], own_tok.at[group], local_sem.at[group]
        )

    def wide(group):
        return pl.ds(pl.multiple_of(group * 2 * rows, 2 * rows), 2 * rows)

    def next_copy(step):
        group = lax.rem(place + step, groups)
        return remote(
            next_tokens.at[:, wide(group)], next_in.at[place],
            next_send.at[step], next_recv.at[place], fsdp=2 * group + side,
        )

    def next_wait(step):
        source = lax.rem(place + groups - step, groups)
        return remote(
            next_tokens.at[:, wide(place)], next_in.at[source],
            next_send.at[step], next_recv.at[source], fsdp=mate,
        )

    def next_local():
        return pltpu.make_async_copy(
            next_tokens.at[:, wide(place)], next_in.at[place], local_sem.at[groups]
        )

    cot_copy().start()
    tok_copy(order(0)[1]).start()
    for step in range(1, groups):
        next_copy(step).start()
    for group in range(groups):
        tok_local(group).start()
    next_local().start()

    def name_rows(pair, carry):
        spots = jnp.concatenate(
            [picks[at, pl.ds(2 * pair + t, 1), :] for t in range(2) for at in range(n_rep)], axis=1
        )
        ids = lax.broadcasted_iota(jnp.int32, (TILE, width), 0)
        pick_row = jnp.where(ids == spots // TILE, 1.0, 0.0).astype(BF16)
        pick_col = jnp.where(ids == lax.rem(spots, TILE), 1.0, 0.0).astype(BF16)
        rows3[pair] = jnp.dot(table[...], pick_row, preferred_element_type=F32).astype(BF16)
        found = jnp.dot(
            table[pl.ds(0, LANES), :], pick_col, preferred_element_type=F32
        )
        first = lax.broadcasted_iota(jnp.int32, (TILE, width), 1) < per_tile
        for part, target in ((found[:TILE], cols_hi), (found[TILE:], cols_lo)):
            target[pair] = jnp.concatenate(
                [jnp.where(first, part, 0.0), jnp.where(first, 0.0, part)], axis=0
            ).astype(BF16)
        return carry

    lax.fori_loop(0, pairs, name_rows, 0, unroll=2)

    def line_copy(way, group, source, target, send, recv):
        return remote(
            source.at[group], target.at[way, group], send.at[group], recv.at[way, group],
            fsdp=lax.rem(me + 2 - 4 * way + n_fsdp, n_fsdp),
        )

    def line_reduce(term, total, source, target, send, recv):
        def copy(way, group):
            return line_copy(way, group, source, target, send, recv)

        def take(way, group):
            copy(way, group).wait_recv()
            total[...] += target[way, group].astype(F32)

        def handle(at, carry):
            way, group = order(at)
            total[...] = term(group, at)

            @pl.when(((way == 0) & (place > 0)) | ((way == 1) & (place < groups - 1)))
            def _():
                take(way, group)

            source[group] = total[...].astype(BF16)

            @pl.when(((way == 0) & (group < groups - 1)) | ((way == 1) & (group > 0)))
            def _():
                copy(way, group + 1 - 2 * way).wait_send()

            copy(way, group).start()
            return carry

        lax.fori_loop(0, groups - 1, handle, 0)
        total[...] = term(place, None)

        @pl.when(place > 0)
        def _():
            take(0, place)

        @pl.when(place < groups - 1)
        def _():
            take(1, place)

    def line_finish(source, target, send, recv):
        @pl.when(place < groups - 1)
        def _():
            line_copy(0, place + 1, source, target, send, recv).wait_send()

        @pl.when(place > 0)
        def _():
            line_copy(1, place - 1, source, target, send, recv).wait_send()

    near[0].wait()
    cot_copy().wait_recv()

    def grad_term(group, at):
        tok_local(group).wait()
        tok_copy(group).wait_recv()
        tok_copy(group).wait_send()
        if at is not None:
            tok_copy(order(at + 1)[1]).start()
        return dot_tn(own_tok[group], cot[...]) + dot_tn(mate_tok[group], mate_cot[...])

    line_reduce(grad_term, acc, line_out, line_in, line_send, line_recv)
    for step in range(0):
        next_copy(step).start()
    near[1].wait()
    vel[...] = decay_rate * moment[...] + acc[...]

    def window(pair):
        top = pl.multiple_of(pair // across * TILE, TILE)
        left = pl.multiple_of(lax.rem(pair, across) * LANES, LANES)
        return pl.ds(top, TILE), pl.ds(left, LANES)

    def coefficients(pair, carry):
        down, over = window(pair)
        head, tail = halves(vel[down, over])
        partly = dot_tn(jnp.concatenate([head, head, tail], axis=0), rows3[pair])
        full = cols_hi[pair].astype(F32) + cols_lo[pair].astype(F32)
        found = jnp.sum(partly * full, axis=0, keepdims=True)
        lane = lax.broadcasted_iota(jnp.int32, (1, width), 1)
        mine = lax.rem(lane, per_tile) // kept == rep
        own_vals[pl.ds(pair, 1), :] = jnp.where(mine, found, 0.0)
        return carry

    lax.fori_loop(0, pairs, coefficients, 0, unroll=8)

    def val_copy(step):
        return remote(
            own_vals, peer_vals.at[step - 1], val_send.at[step], val_recv.at[step],
            rep=lax.rem(rep + step, n_rep),
        )

    for step in range(1, n_rep):
        val_copy(step).start()

    def inverse(pair, values):
        row_parts = rows3[pair]
        scaled = (row_parts[:TILE].astype(F32) + row_parts[TILE:LANES].astype(F32)) * values
        head, tail = halves(scaled)
        both = dot_nt(jnp.concatenate([head, tail], axis=0), cols_hi[pair])
        return both[:TILE] + both[TILE:] + dot_nt(head, cols_lo[pair])

    def residual(pair, carry):
        down, over = window(pair)
        moment_out[0, down, over] = vel[down, over] - inverse(pair, own_vals[pl.ds(pair, 1), :])
        return carry

    lax.fori_loop(0, pairs // 2, residual, 0, unroll=8)

    near[2].wait()
    for step in range(1, n_rep):
        val_copy(step).wait_recv()

    def renew_half(which):
        def renew(at, carry):
            pair = which * (pairs // 2) + at
            down, over = window(pair)
            values = own_vals[pl.ds(pair, 1), :]
            for step in range(1, n_rep):
                values += peer_vals[step - 1, pl.ds(pair, 1), :]
            new_weight[side, down, over] = (
                weight[down, over].astype(F32) - step_size * inverse(pair, values)
            ).astype(BF16)
            return carry

        lax.fori_loop(0, pairs // 2, renew, 0, unroll=8)

    def half_rows(owner_side, which):
        return new_weight.at[owner_side, pl.ds(pl.multiple_of(which * half, half), half)]

    def half_copy():
        return remote(
            half_rows(side, core), half_rows(side, core),
            half_send.at[0], half_recv.at[0], fsdp=mate,
        )

    def half_wait():
        return remote(
            half_rows(1 - side, core), half_rows(1 - side, core),
            half_send.at[0], half_recv.at[0], fsdp=mate,
        )

    def pass_copy():
        return remote(
            half_rows(1 - side, core), half_rows(1 - side, core),
            half_send.at[1], half_recv.at[1], rep=sibling,
        )

    def pass_wait():
        return remote(
            half_rows(1 - side, 1 - core), half_rows(1 - side, 1 - core),
            half_send.at[1], half_recv.at[1], rep=sibling,
        )

    renew_half(core)
    half_copy().start()
    renew_half(1 - core)
    lax.fori_loop(pairs // 2, pairs, residual, 0, unroll=8)
    half_wait().wait_recv()
    pass_copy().start()
    next_local().wait()
    for step in range(1, groups):
        next_wait(step).wait_recv()
    pass_wait().wait_recv()

    def key_term(group, at):
        return jnp.dot(
            next_in[group, :, pl.ds(0, rows)], new_weight[0], preferred_element_type=F32
        ) + jnp.dot(
            next_in[group, :, pl.ds(rows, rows)], new_weight[1], preferred_element_type=F32
        )

    line_reduce(key_term, keys_out, key_out, key_in, key_send, key_recv)

    cot_copy().wait_send()
    for step in range(1, groups):
        next_copy(step).wait_send()
    for step in range(1, n_rep):
        val_copy(step).wait_send()
    half_copy().wait_send()
    pass_copy().wait_send()
    line_finish(line_out, line_in, line_send, line_recv)
    line_finish(key_out, key_in, key_send, key_recv)


def on_device(n_rep, n_fsdp, tokens, cotangent, momentum, weight, picks, next_tokens):
    groups = n_fsdp // 2
    rows, cols = weight.shape
    count = tokens.shape[0]
    ahead = next_tokens.shape[0]
    tiles, kept = picks.shape[1:]
    pairs, width = tiles // 2, 2 * n_rep * kept
    dma = pltpu.SemaphoreType.DMA
    vmem = pl.BlockSpec(memory_space=pltpu.VMEM)
    hbm = pl.BlockSpec(memory_space=pl.ANY)
    return pl.pallas_call(
        functools.partial(kernel, n_rep, n_fsdp),
        out_shape=(
            jax.ShapeDtypeStruct(momentum.shape, F32),
            jax.ShapeDtypeStruct((ahead, cols), F32),
        ),
        in_specs=[hbm, hbm, hbm, hbm, vmem, hbm, vmem],
        out_specs=(vmem, vmem),
        scratch_shapes=[
            pltpu.VMEM((count, cols), BF16),
            pltpu.VMEM((rows, cols), F32),
            pltpu.VMEM((rows, cols), BF16),
            pltpu.VMEM((groups, count, rows), BF16),
            pltpu.VMEM((groups, count, rows), BF16),
            pltpu.VMEM((count, cols), BF16),
            pltpu.VMEM((2, groups, rows, cols), BF16),
            pltpu.VMEM((groups, rows, cols), BF16),
            pltpu.VMEM((rows, cols), F32),
            pltpu.VMEM((rows, cols), F32),
            pltpu.VMEM((pairs, 3 * TILE, width), BF16),
            pltpu.VMEM((pairs, LANES, width), BF16),
            pltpu.VMEM((pairs, LANES, width), BF16),
            pltpu.VMEM((pairs, width), F32),
            pltpu.VMEM((n_rep - 1, pairs, width), F32),
            pltpu.VMEM((2, rows, cols), BF16),
            pltpu.VMEM((groups, ahead, 2 * rows), BF16),
            pltpu.VMEM((2, groups, ahead, cols), BF16),
            pltpu.VMEM((groups, ahead, cols), BF16),
            dma((3,)),
            dma((groups + 1,)),
            dma((2,)),
            dma((groups,)),
            dma((groups,)),
            dma((groups,)),
            dma((2, groups)),
            dma((n_rep,)),
            dma((n_rep,)),
            dma((groups,)),
            dma((groups,)),
            dma((2,)),
            dma((2,)),
            dma((groups,)),
            dma((2, groups)),
        ],
        compiler_params=pltpu.CompilerParams(
            collective_id=0, has_side_effects=True, vmem_limit_bytes=52 * 1024 * 1024
        ),
    )(tokens, cotangent, momentum, weight, picks, next_tokens, jnp.asarray(cosine_parts()))


def solution(mesh):
    placed = (
        P(("rep", "fsdp"), None),
        P(("rep", "fsdp"), None),
        P("rep", "fsdp", None),
        P("fsdp", None),
        P(None, "fsdp", None),
        P(("rep", "fsdp"), None),
    )
    return jax.shard_map(
        functools.partial(on_device, mesh.shape["rep"], mesh.shape["fsdp"]),
        mesh=mesh,
        in_specs=placed,
        out_specs=(P("rep", "fsdp", None), P(("rep", "fsdp"), None)),
        check_vma=False,
    )
```
